32 devices in a mesh: slab: 4 (over y, core), trace: 8 (over z, x).
Axes of the slice: x: 2, y: 2, z: 4, core: 2. Of those that a mesh axis runs over, the one named last changes fastest.
Arguments:
- near_tiles: float32 [4, 2, 2, 768, 6144], P('slab', None, None, None, 'trace'), may hold values from -0.078125 to 0.078125
- near_side: int32 [4, 8], P('slab', 'trace'), may hold values from -1 to 1, as said below
- skeleton: int32 [4, 8, 64], P('slab', 'trace'), may hold values from 0 to 767, as said below
- far_coupling: float32 [4, 2, 512, 512], P('slab', None, 'trace'), may hold values from -0.125 to 0.125
- far_basis: float32 [4, 2, 64, 6144], P('slab', None, None, 'trace'), may hold values from -0.5 to 0.5
- sources: float32 [4, 2, 1, 16, 6144], P('slab', None, None, None, 'trace'), may hold values from -200 to 200
Outputs:
- traces: float32 [4, 2, 1, 16, 6144], P('slab', None, None, None, 'trace')
The draws below stay inside these ranges and needn't reach their ends.
Inputs may be any that keep to these rules, and one draw needn't show every extreme that they name: `near_side`: each entry is -1 or 1, so that the second near tile lies in a block next to the row's own block; it is 1 for the first block and -1 for the last. `skeleton`: the 64 positions of one block are distinct.
All inputs are finite; a program needn't handle non-finite values.
Results may differ from the reference program's by a relative error of at most 0.0001.
Values sent between devices are 32-bit elements; how exact they have to be, the bound alone decides.
No kernel may reach another device: no remote copies, remote signals or barrier semaphores. Data moves between devices by JAX's collectives and lax.ppermute only.
A program may use at most 128 MiB of HBM per device.

```python
import math
import jax
import jax.numpy as jnp
from jax import lax

TILE = 768
RANK = 64
NEAR = 2
MB = 1
B = 16
BLOCKS = 8
N = 6144
N_SLAB = 4


def draw_near_side(key, part):
    coin = jax.random.randint(key, (N_SLAB, BLOCKS), 0, 2).astype(jnp.int32)
    offsets = 2 * coin - 1
    column = jnp.arange(BLOCKS, dtype=jnp.int32)[None, :]
    offsets = jnp.where(column == 0, 1, offsets)
    offsets = jnp.where(column == BLOCKS - 1, -1, offsets)
    return offsets.astype(jnp.int32)


def draw_skeleton(key, part):
    scores = jax.random.randint(key, (N_SLAB, BLOCKS, TILE), 0, 1 << 20).astype(jnp.int32) * TILE + jnp.arange(TILE, dtype=jnp.int32)
    order = jnp.argsort(scores, axis=-1)
    return order[..., :RANK].astype(jnp.int32)


def draw_sources(key, part):
    key_col, key_row, key_base = jax.random.split(key, 3)
    position = jnp.arange(N, dtype=jnp.float32) / N
    rough = jnp.exp(jax.random.uniform(key_col, (N_SLAB, 1, 1, 1, N), jnp.float32, 0.0, math.log(3.3)))
    col_scale = jnp.power(3.0, position) * rough
    row_scale = jnp.exp(jax.random.uniform(key_row, (N_SLAB, 1, MB, B, 1), jnp.float32, 0.0, math.log(5.0)))
    shape_all = (N_SLAB, 2, MB, B, N)
    base = jnp.clip(jax.random.normal(key_base, shape_all, jnp.float32), -4.0, 4.0)
    return (base * col_scale * row_scale).astype(jnp.float32)


def levels(key, dims, cuts, least, high):
    gain = 1.0
    for dim, parts in cuts:
        heights = jax.random.uniform(jax.random.fold_in(jax.random.fold_in(key, 6), dim), (parts,), jnp.float32, least / len(cuts), high / len(cuts))
        gain = gain * jnp.repeat(jnp.exp(heights), dims[dim] // parts).reshape((-1,) + (1,) * (len(dims) - 1 - dim))
    return gain


def centred(stream_key, dims, deviation, limit, cuts=(), kind=jnp.bfloat16):
    loudness = levels(stream_key, dims, cuts, -0.22, 0.18) if cuts else 1.0
    drawn = jax.random.normal(stream_key, dims, jnp.float32) * deviation * loudness
    return jnp.minimum(jnp.maximum(drawn, -limit), limit).astype(kind)


def setup_inputs(seed: int = 0) -> dict:
    streams_of = jax.random.split(jax.random.key(seed), 7)
    near_tiles = centred(streams_of[0], (N_SLAB, NEAR, 2, TILE, N), (4 * NEAR * TILE) ** -0.5, 0.078125, ((0, 4), (4, 8)), jnp.float32)
    near_side = draw_near_side(jax.random.fold_in(streams_of[6], 71), 0)
    skeleton = draw_skeleton(jax.random.fold_in(streams_of[6], 71), 0)
    far_coupling = centred(streams_of[3], (N_SLAB, 2, BLOCKS * RANK, BLOCKS * RANK), (4 * BLOCKS * RANK) ** -0.5, 0.125, ((0, 4), (2, 8)), jnp.float32)
    far_basis = centred(streams_of[4], (N_SLAB, 2, RANK, N), (2 * RANK) ** -0.5, 0.5, ((0, 4), (3, 8)), jnp.float32)
    sources = draw_sources(jax.random.fold_in(streams_of[6], 71), 0)
    return {"near_tiles": near_tiles, "near_side": near_side, "skeleton": skeleton, "far_coupling": far_coupling, "far_basis": far_basis, "sources": sources}


exact_mode = lax.Precision.HIGHEST
small_eps = 1e-06

def block_product(form, left_re, left_im, right_re, right_im):
    real_part = jnp.einsum(form, left_re, right_re, precision=exact_mode) - jnp.einsum(form, left_im, right_im, precision=exact_mode)
    imag_part = jnp.einsum(form, left_re, right_im, precision=exact_mode) + jnp.einsum(form, left_im, right_re, precision=exact_mode)
    return (real_part, imag_part)

def reference(near_tiles, near_side, skeleton, far_coupling, far_basis, sources):
    row_count = MB * B
    block_ids = jnp.arange(BLOCKS, dtype=jnp.int32)
    owner_ids = jnp.arange(BLOCKS * RANK, dtype=jnp.int32) // RANK
    trace_in = jnp.zeros((2, row_count, BLOCKS, TILE), jnp.float32)
    results = []
    for slab_idx in range(N_SLAB):
        tile_set = near_tiles[slab_idx].reshape(NEAR, 2, TILE, BLOCKS, TILE)
        offsets = near_side[slab_idx].astype(jnp.int32)
        beside_in = jnp.take(trace_in, block_ids + offsets, axis=2)
        own_re, own_im = block_product('abi,ibo->abo', trace_in[0], trace_in[1], tile_set[0, 0], tile_set[0, 1])
        next_re, next_im = block_product('abi,ibo->abo', beside_in[0], beside_in[1], tile_set[1, 0], tile_set[1, 1])
        picked = jnp.take_along_axis(trace_in, skeleton[slab_idx][None, None], axis=3).reshape(2, row_count, BLOCKS * RANK)
        keep_mask = ((owner_ids[None, :] != block_ids[:, None]) & (owner_ids[None, :] != (block_ids + offsets)[:, None])).astype(jnp.float32)
        masked = picked[:, :, None, :] * keep_mask[None, None]
        coupling = far_coupling[slab_idx].reshape(2, BLOCKS, RANK, BLOCKS * RANK)
        coef_re, coef_im = block_product('abj,bkj->abk', masked[0], masked[1], coupling[0], coupling[1])
        basis = far_basis[slab_idx].reshape(2, RANK, BLOCKS, TILE)
        far_re, far_im = block_product('abk,kbo->abo', coef_re, coef_im, basis[0], basis[1])
        source = sources[slab_idx].reshape(2, row_count, BLOCKS, TILE)
        updated = jnp.stack([own_re + next_re + far_re, own_im + next_im + far_im]) + source
        trace_in = updated
        energy = lax.optimization_barrier(jnp.sum(updated * updated, axis=(0, 2, 3))) / (2 * BLOCKS * TILE)
        normed = updated / jnp.sqrt(energy + small_eps)[None, :, None, None]
        results.append(normed.reshape(2, MB, B, BLOCKS * TILE))
    return jnp.stack(results)
```

```python
import jax
import jax.numpy as jnp
from jax import lax
from jax.experimental import pallas as pl
from jax.experimental.pallas import tpu as pltpu
from jax.sharding import PartitionSpec as P

f32 = jnp.float32
bf16 = jnp.bfloat16
small_eps = 1e-06
both_axes = ("slab", "trace")
in_vmem = pl.BlockSpec(memory_space=pltpu.VMEM)
in_smem = pl.BlockSpec(memory_space=pltpu.SMEM)
vmem_room = pltpu.CompilerParams(vmem_limit_bytes=20 << 20)


def two_parts(x):
    high = x.astype(bf16)
    return high, (x - high.astype(f32)).astype(bf16)


def three_parts(x):
    high = x.astype(bf16)
    rest = x - high.astype(f32)
    middle = rest.astype(bf16)
    return high, middle, (rest - middle.astype(f32)).astype(bf16)


def dot(a, b):
    return jnp.dot(a, b, preferred_element_type=f32)


def times(stacked, high, weight_high, weight_low):
    rows = high.shape[0]
    both = dot(stacked, weight_high)
    return both[:rows] + both[rows:] + dot(high, weight_low)


def complex_times(x, weights):
    high, low = two_parts(x)
    stacked = jnp.concatenate([high, low], axis=0)
    by_re = times(stacked, high, *weights[0])
    by_im = times(stacked, high, *weights[1])
    half = x.shape[0] // 2
    return by_re[:half] - by_im[half:], by_im[:half] + by_re[half:]


def pick(x, skel_row):
    width = x.shape[1]
    count = skel_row.shape[1]
    rows = lax.broadcasted_iota(jnp.int32, (width, count), 0)
    chosen = jnp.where(rows == skel_row, 1.0, 0.0).astype(bf16)
    parts = three_parts(x)
    n = x.shape[0]
    out = dot(jnp.concatenate(parts, axis=0), chosen)
    return out[:n] + (out[n : 2 * n] + out[2 * n :])


def put_state(state_ref, small_ref, x, skel_row):
    n, width = x.shape
    half = n // 2
    rank = skel_row.shape[1]
    chosen = pick(x, skel_row)
    state_ref[:, :width] = x
    state_ref[:, width:] = jnp.concatenate(
        [chosen, jnp.zeros((n, state_ref.shape[1] - width - rank), f32)], axis=1
    )
    small_ref[...] = jnp.concatenate([chosen[:half], chosen[half:]], axis=1)


def first_kernel(skel_ref, src_ref, state_ref, small_ref):
    put_state(state_ref, small_ref, src_ref[...], skel_ref[...])


def split_kernel(tiles_ref, high_ref, low_ref):
    plane = pl.program_id(0)
    high, low = two_parts(tiles_ref[0])
    high_ref[plane] = high
    low_ref[plane] = low


def far_split_kernel(side_ref, coupling_ref, basis_ref, coef_ref, base_ref):
    blocks = lax.axis_size("trace")
    here = lax.axis_index("trace")
    _, rank, total = coupling_ref.shape
    turned = lax.rem((blocks - here) * rank, total)
    position = lax.broadcasted_iota(jnp.int32, (rank, total), 1)
    ahead = side_ref[0, 0] > 0
    start = jnp.where(ahead, rank, total - rank)
    keep = (position < start) | (position >= start + rank)
    for part in range(2):
        rolled = jnp.where(keep, pltpu.roll(coupling_ref[part], turned, 1), 0.0)
        high, low = two_parts(rolled.T)
        coef_ref[part, 0] = high
        coef_ref[part, 1] = low
        high, low = two_parts(basis_ref[part])
        base_ref[part, 0] = high
        base_ref[part, 1] = low


def near_kernel(step, side_ref, own_ref, before_ref, after_ref, src_ref, high_ref, low_ref, out_ref):
    @pl.when(lax.axis_index("slab") == step)
    def _():
        n, width = src_ref.shape
        half = n // 2
        ahead = side_ref[0, 0] > 0
        beside = jnp.where(ahead, after_ref[:, :width], before_ref[:, :width])
        total_re, total_im = src_ref[:half], src_ref[half:]
        for slot, x in ((0, own_ref[:, :width]), (1, beside)):
            weights = [(high_ref[2 * slot + p], low_ref[2 * slot + p]) for p in range(2)]
            re, im = complex_times(x, weights)
            total_re += re
            total_im += im
        out_ref[:half] = total_re
        out_ref[half:] = total_im


def far_kernel(step, skel_ref, old_ref, near_ref, before_ref, after_ref, *refs):
    *small_refs, coef_ref, base_ref, state_ref, small_ref = refs
    active = lax.axis_index("slab") == step

    @pl.when(active)
    def _():
        n, width = near_ref.shape
        half = n // 2
        rank = skel_ref.shape[1]
        pieces = [after_ref[:, width : width + rank]]
        for ref in small_refs:
            pieces.append(jnp.concatenate([ref[:, :rank], ref[:, rank:]], axis=0))
        pieces.append(before_ref[:, width : width + rank])
        values = jnp.concatenate(pieces, axis=1)
        weights = [(coef_ref[p, 0, rank:], coef_ref[p, 1, rank:]) for p in range(2)]
        coef = jnp.concatenate(complex_times(values, weights), axis=0)
        weights = [(base_ref[p, 0], base_ref[p, 1]) for p in range(2)]
        far = jnp.concatenate(complex_times(coef, weights), axis=0)
        put_state(state_ref, small_ref, near_ref[...] + far, skel_ref[...])

    @pl.when(jnp.logical_not(active))
    def _():
        width = near_ref.shape[1]
        rank = skel_ref.shape[1]
        half = near_ref.shape[0] // 2
        state_ref[...] = old_ref[...]
        small_ref[...] = jnp.concatenate(
            [old_ref[:half, width : width + rank], old_ref[half:, width : width + rank]], axis=1
        )


def energy_kernel(state_ref, out_ref):
    half = state_ref.shape[0] // 2
    width = state_ref.shape[1] - 128
    x = state_ref[:, :width]
    squares = x * x
    each = jnp.sum(squares[:half] + squares[half:], axis=1, keepdims=True)
    lanes = jnp.broadcast_to(each, (half, 128)).T
    out_ref[...] = jnp.broadcast_to(lanes[:1], out_ref.shape)


def norm_kernel(count, state_ref, sums_ref, out_ref):
    half = state_ref.shape[0] // 2
    width = out_ref.shape[-1]
    total = jnp.sum(sums_ref[...], axis=0, keepdims=True)
    scale = jnp.broadcast_to(1.0 / jnp.sqrt(total / count + small_eps), (128, half)).T[:, :1]
    out_ref[0] = state_ref[:half, :width] * scale
    out_ref[1] = state_ref[half:, :width] * scale


def ring_pairs(step, shift, slabs, blocks):
    pairs = []
    for place in range(slabs):
        source = (step - 1 + place) % slabs
        target = (source + 1) % slabs
        move = shift if place == 0 else 0
        pairs += [
            (source * blocks + c, target * blocks + (c + move) % blocks) for c in range(blocks)
        ]
    return pairs


def on_device(near_tiles, near_side, skeleton, far_coupling, far_basis, sources):
    slabs = lax.axis_size("slab")
    blocks = lax.axis_size("trace")
    _, slots, parts, tile, width = near_tiles.shape
    _, _, batches, shots, _ = sources.shape
    rank = skeleton.shape[2]
    rows = batches * shots
    n = parts * rows
    wide = width + 128

    src = sources.reshape(n, width)
    tiles = near_tiles.reshape(slots * parts, tile, width)
    skel_here = skeleton.reshape(1, rank)
    skel_next = lax.ppermute(
        skel_here, "slab", [((s + 1) % slabs, s) for s in range(slabs)]
    )
    state_type = jax.ShapeDtypeStruct((n, wide), f32)
    small_type = jax.ShapeDtypeStruct((rows, parts * rank), f32)
    state, small = pl.pallas_call(
        first_kernel,
        out_shape=(state_type, small_type),
        in_specs=[in_vmem] * 2,
        out_specs=[in_vmem] * 2,
        compiler_params=vmem_room,
        name="first",
    )(skel_next, src)
    halves = jax.ShapeDtypeStruct(tiles.shape, bf16)
    tiles_high, tiles_low = pl.pallas_call(
        split_kernel,
        grid=(slots * parts,),
        out_shape=(halves, halves),
        in_specs=[pl.BlockSpec((1, tile, width), lambda i: (i, 0, 0))],
        out_specs=[in_vmem] * 2,
        compiler_params=vmem_room,
        name="split_tiles",
    )(tiles)
    coef, base = pl.pallas_call(
        far_split_kernel,
        out_shape=(
            jax.ShapeDtypeStruct((parts, 2, blocks * rank, rank), bf16),
            jax.ShapeDtypeStruct((parts, 2, rank, width), bf16),
        ),
        in_specs=[in_smem, in_vmem, in_vmem],
        out_specs=[in_vmem] * 2,
        compiler_params=vmem_room,
        name="split_far",
    )(near_side, far_coupling[0], far_basis[0])

    for step in range(1, slabs):

        def send(x, shift):
            return lax.ppermute(x, both_axes, ring_pairs(step, shift, slabs, blocks))

        own = send(state, 0)
        before = send(state, 1)
        after = send(state, blocks - 1)
        smalls = [send(small, shift) for shift in range(blocks - 2, 1, -1)]
        near = pl.pallas_call(
            lambda *refs, step=step: near_kernel(step, *refs),
            out_shape=jax.ShapeDtypeStruct((n, width), f32),
            in_specs=[in_smem] + [in_vmem] * 6,
            out_specs=in_vmem,
            compiler_params=vmem_room,
            name="near",
        )(near_side, own, before, after, src, tiles_high, tiles_low)
        state, small = pl.pallas_call(
            lambda *refs, step=step: far_kernel(step, *refs),
            out_shape=(state_type, small_type),
            in_specs=[in_vmem] * (7 + len(smalls)),
            out_specs=[in_vmem] * 2,
            compiler_params=vmem_room,
            name="far",
        )(skel_next, state, near, before, after, *smalls, coef, base)

    partial = pl.pallas_call(
        energy_kernel,
        out_shape=jax.ShapeDtypeStruct((blocks, rows), f32),
        in_specs=[in_vmem],
        out_specs=in_vmem,
        compiler_params=vmem_room,
        name="energy",
    )(state)
    sums = lax.all_to_all(partial, "trace", 0, 0)
    normed = pl.pallas_call(
        lambda *refs: norm_kernel(float(parts * width * blocks), *refs),
        out_shape=jax.ShapeDtypeStruct((parts, rows, width), f32),
        in_specs=[in_vmem] * 2,
        out_specs=in_vmem,
        compiler_params=vmem_room,
        name="norm",
    )(state, sums)
    return normed.reshape(sources.shape)


def solution(mesh):
    placed = (
        P("slab", None, None, None, "trace"),
        P("slab", "trace"),
        P("slab", "trace", None),
        P("slab", None, "trace", None),
        P("slab", None, None, "trace"),
        P("slab", None, None, None, "trace"),
    )
    return jax.shard_map(
        on_device,
        mesh=mesh,
        in_specs=placed,
        out_specs=P("slab", None, None, None, "trace"),
        check_vma=False,
    )
```

```python
import jax
import jax.numpy as jnp
from jax import lax
from jax.experimental import pallas as pl
from jax.experimental.pallas import tpu as pltpu
from jax.sharding import PartitionSpec as P

f32 = jnp.float32
bf16 = jnp.bfloat16
small_eps = 1e-06
both_axes = ("slab", "trace")
in_vmem = pl.BlockSpec(memory_space=pltpu.VMEM)
in_smem = pl.BlockSpec(memory_space=pltpu.SMEM)

pieces = 4


def two_parts(x):
    high = x.astype(bf16)
    return high, (x - high.astype(f32)).astype(bf16)


def three_parts(x):
    high = x.astype(bf16)
    rest = x - high.astype(f32)
    middle = rest.astype(bf16)
    return high, middle, (rest - middle.astype(f32)).astype(bf16)


def dot(a, b):
    return jnp.dot(a, b, preferred_element_type=f32)


def times(stacked, high, weight_high, weight_low):
    rows = high.shape[0]
    both = dot(stacked, weight_high)
    return both[:rows] + both[rows:] + dot(high, weight_low)


def complex_times(x, weights):
    high, low = two_parts(x)
    stacked = jnp.concatenate([high, low], axis=0)
    by_re = times(stacked, high, *weights[0])
    by_im = times(stacked, high, *weights[1])
    half = x.shape[0] // 2
    return by_re[:half] - by_im[half:], by_im[:half] + by_re[half:]


def on_odd():
    return lax.rem(lax.axis_index("trace"), 2) == 1


def pick(x, skel_row):
    n, width = x.shape
    rank = skel_row.shape[1]
    rows = lax.broadcasted_iota(jnp.int32, (width, rank), 0)
    chosen = jnp.where(rows == skel_row, 1.0, 0.0).astype(bf16)
    out = dot(jnp.concatenate(three_parts(x), axis=0), chosen)
    out = out[:n] + (out[n : 2 * n] + out[2 * n :])
    lane = lax.broadcasted_iota(jnp.int32, (n, 2 * rank), 1)
    return jnp.where((lane >= rank) == on_odd(), jnp.concatenate([out, out], axis=1), 0.0)


def first_kernel(skel_ref, src_ref, small_ref):
    small_ref[...] = pick(src_ref[...], skel_ref[...])


def split_tiles(slot, tiles_ref, half_refs, held_ref, sems, meanwhile):
    pieces_all, rows, _ = held_ref.shape
    _, tile, _ = tiles_ref.shape
    per = tile // rows
    copies = [
        pltpu.make_async_copy(
            tiles_ref.at[slot * (pieces_all // per) + i // per, pl.ds(i % per * rows, rows)],
            held_ref.at[i],
            sems.at[i],
        )
        for i in range(pieces_all)
    ]
    for copy in copies:
        copy.start()
    meanwhile()
    high_ref, low_ref = half_refs
    for i, copy in enumerate(copies):
        copy.wait()
        high, low = two_parts(held_ref[i])
        place = pl.ds(i % per * rows, rows)
        high_ref[i // per, place] = high
        low_ref[i // per, place] = low


def split_far_kernel(side_ref, coupling_in, basis_in, tiles_ref, *refs):
    coef_ref, base_ref, *half_refs, coupling_ref, basis_ref, far_sems, held_ref, sems = refs
    far_copies = [
        pltpu.make_async_copy(coupling_in, coupling_ref, far_sems.at[0]),
        pltpu.make_async_copy(basis_in, basis_ref, far_sems.at[1]),
    ]
    for copy in far_copies:
        copy.start()

    def meanwhile():
        for copy in far_copies:
            copy.wait()
        split_far(side_ref, coupling_ref, basis_ref, coef_ref, base_ref)

    split_tiles(0, tiles_ref, half_refs, held_ref, sems, meanwhile)


def split_kernel(tiles_ref, high_ref, low_ref, held_ref, sems):
    split_tiles(1, tiles_ref, (high_ref, low_ref), held_ref, sems, lambda: None)


def split_far(side_ref, coupling_ref, basis_ref, coef_ref, base_ref):
    here = lax.axis_index("trace")
    _, rank, total = coupling_ref.shape
    width = 2 * rank
    half = lax.broadcasted_iota(jnp.int32, (rank, width), 1) // rank
    for j in range(total // width):
        group = (here // 2) ^ j
        block = group * 2 + half
        keep = (block != here) & (block != here + side_ref[0, 0])
        place = pl.ds(pl.multiple_of(group * width, width), width)
        for part in range(2):
            high, low = two_parts(jnp.where(keep, coupling_ref[part, :, place], 0.0).T)
            coef_ref[part, 0, j * width : (j + 1) * width] = high
            coef_ref[part, 1, j * width : (j + 1) * width] = low
    for part in range(2):
        high, low = two_parts(basis_ref[part])
        base_ref[part, 0] = high
        base_ref[part, 1] = low


def add_near(out_ref, start, x, high_ref, low_ref):
    half = x.shape[0] // 2
    re, im = complex_times(x, [(high_ref[p], low_ref[p]) for p in range(2)])
    out_ref[:half] = start[:half] + re
    out_ref[half:] = start[half:] + im


def own_kernel(step, own_ref, src_ref, high_ref, low_ref, out_ref):
    @pl.when(lax.axis_index("slab") == step)
    def _():
        add_near(out_ref, src_ref[...], own_ref[...], high_ref, low_ref)


def beside_kernel(step, side_ref, mate_ref, other_ref, start_ref, high_ref, low_ref, out_ref):
    @pl.when(lax.axis_index("slab") == step)
    def _():
        width = start_ref.shape[1]
        mate = (side_ref[0, 0] < 0) == on_odd()
        x = jnp.where(mate, mate_ref[:, :width], other_ref[:, :width])
        add_near(out_ref, start_ref[...], x, high_ref, low_ref)


def far_kernel(step, skel_ref, old_ref, near_ref, mate_ref, *refs):
    *pair_refs, coef_ref, base_ref, state_ref, small_ref = refs
    active = lax.axis_index("slab") == step
    width = near_ref.shape[1]

    @pl.when(active)
    def _():
        values = [ref[...] for ref in pair_refs]
        values = jnp.concatenate([mate_ref[:, width:]] + values, axis=1)
        weights = [(coef_ref[p, 0], coef_ref[p, 1]) for p in range(2)]
        coef = jnp.concatenate(complex_times(values, weights), axis=0)
        weights = [(base_ref[p, 0], base_ref[p, 1]) for p in range(2)]
        far = jnp.concatenate(complex_times(coef, weights), axis=0)
        new = near_ref[...] + far
        state_ref[...] = new
        small_ref[...] = pick(new, skel_ref[...])

    @pl.when(jnp.logical_not(active))
    def _():
        state_ref[...] = old_ref[...]
        small_ref[...] = jnp.zeros_like(small_ref)


def energy_kernel(state_ref, out_ref):
    half = state_ref.shape[0] // 2
    squares = state_ref[...] * state_ref[...]
    each = jnp.sum(squares[:half] + squares[half:], axis=1, keepdims=True)
    out_ref[...] = jnp.broadcast_to(jnp.broadcast_to(each, (half, 128)).T[:1], out_ref.shape)


def norm_kernel(count, state_ref, sums_ref, out_ref):
    half = state_ref.shape[0] // 2
    total = jnp.sum(sums_ref[...], axis=0, keepdims=True)
    scale = jnp.broadcast_to(1.0 / jnp.sqrt(total / count + small_eps), (128, half)).T[:, :1]
    out_ref[0] = state_ref[:half] * scale
    out_ref[1] = state_ref[half:] * scale


def about(us):
    return pl.CostEstimate(
        flops=int(us * 1.15e9), bytes_accessed=int(us * 3.69e6), transcendentals=0
    )


def across(c, blocks):
    return min(max((c ^ 1) + (2 if c % 2 else -2), 0), blocks - 1)


def call(kernel, name, outs, specs, args, room=6, **more):
    many = isinstance(outs, tuple)
    return pl.pallas_call(
        kernel,
        out_shape=outs,
        in_specs=specs,
        out_specs=[in_vmem] * len(outs) if many else in_vmem,
        compiler_params=pltpu.CompilerParams(vmem_limit_bytes=room << 20),
        name=name,
        **more,
    )(*args)


in_hbm = pl.BlockSpec(memory_space=pl.ANY)


def far_from(x):
    return pltpu.with_memory_space_constraint(x, pltpu.HBM)


def ring_pairs(step, move, slabs, blocks):
    pairs = []
    for place in range(slabs):
        source = (step - 1 + place) % slabs
        target = (source + 1) % slabs
        for c in range(blocks):
            pairs.append((source * blocks + c, target * blocks + (move(c) if place == 0 else c)))
    return pairs


def on_device(near_tiles, near_side, skeleton, far_coupling, far_basis, sources):
    slabs = lax.axis_size("slab")
    blocks = lax.axis_size("trace")
    _, slots, parts, tile, width = near_tiles.shape
    _, _, batches, shots, _ = sources.shape
    rank = skeleton.shape[2]
    rows = batches * shots
    n = parts * rows
    state_type = jax.ShapeDtypeStruct((n, width), f32)
    small_type = jax.ShapeDtypeStruct((n, 2 * rank), f32)

    src = sources.reshape(n, width)
    skel_next = lax.ppermute(
        skeleton.reshape(1, rank), "slab", [((s + 1) % slabs, s) for s in range(slabs)]
    )
    halves = jax.ShapeDtypeStruct((parts, tile, width), bf16)

    held = [
        pltpu.VMEM((parts * pieces, tile // pieces, width), f32),
        pltpu.SemaphoreType.DMA((parts * pieces,)),
    ]

    def split_first(planes):
        coef, base, *own_halves = call(
            split_far_kernel,
            "split_own",
            (
                jax.ShapeDtypeStruct((parts, 2, blocks * rank, rank), bf16),
                jax.ShapeDtypeStruct((parts, 2, rank, width), bf16),
                halves,
                halves,
            ),
            [in_smem] + [in_hbm] * 3,
            (near_side, far_from(far_coupling[0]), far_from(far_basis[0]), far_from(planes)),
            scratch_shapes=[
                pltpu.VMEM(far_coupling.shape[1:], f32),
                pltpu.VMEM(far_basis.shape[1:], f32),
                pltpu.SemaphoreType.DMA((2,)),
                *held,
            ],
            cost_estimate=about(2.5),
            room=12,
        )
        return coef, base, own_halves

    def split_second(planes):
        return call(
            split_kernel,
            "split_beside",
            (halves, halves),
            [in_hbm],
            (far_from(planes),),
            scratch_shapes=held,
            cost_estimate=about(2.5),
            room=12,
        )

    planes = near_tiles.reshape(slots * parts, tile, width)
    coef, base, own_halves = split_first(planes)
    skel_next, coef = lax.optimization_barrier((skel_next, coef))
    state = src
    small = call(first_kernel, "first", small_type, [in_vmem] * 2, (skel_next, src))
    state, small = lax.optimization_barrier((state, small))

    for step in range(1, slabs):

        def send(x, move):
            return lax.ppermute(x, both_axes, ring_pairs(step, move, slabs, blocks))

        def send_pair(x, j):
            return send(x, lambda c: c ^ (2 * j))

        swapped = lax.ppermute(small, "trace", [(c, c ^ 1) for c in range(blocks)])
        pair = small + swapped
        own = send(state, lambda c: c)
        if step == 1:
            own, planes = lax.optimization_barrier((own, planes))
            beside_halves = split_second(planes)
        wide = jnp.concatenate([state, small], axis=1)
        ways = range(1, blocks // 2)
        mate = send(wide, lambda c: c ^ 1)
        other = send(state, lambda c: across(c, blocks))
        by_way = {j: send_pair(pair, j) for j in reversed(ways)}
        pairs = [by_way[j] for j in ways]
        near = call(
            lambda *refs, step=step: own_kernel(step, *refs),
            "own",
            state_type,
            [in_vmem] * 4,
            (own, src, *own_halves),
            cost_estimate=about(5),
        )
        near = call(
            lambda *refs, step=step: beside_kernel(step, *refs),
            "beside",
            state_type,
            [in_smem] + [in_vmem] * 5,
            (near_side, mate, other, near, *beside_halves),
            cost_estimate=about(0.85),
        )
        args = (skel_next, state, near, mate, *pairs, coef, base)
        state, small = call(
            lambda *refs, step=step: far_kernel(step, *refs),
            "far",
            (state_type, small_type),
            [in_vmem] * len(args),
            args,
            cost_estimate=about(0.7),
        )

    partial = call(
        energy_kernel, "energy", jax.ShapeDtypeStruct((blocks, rows), f32), [in_vmem], (state,)
    )
    sums = lax.all_to_all(partial, "trace", 0, 0)
    normed = call(
        lambda *refs: norm_kernel(float(parts * width * blocks), *refs),
        "norm",
        jax.ShapeDtypeStruct((parts, rows, width), f32),
        [in_vmem] * 2,
        (state, sums),
    )
    return normed.reshape(sources.shape)


def solution(mesh):
    placed = (
        P("slab", None, None, None, "trace"),
        P("slab", "trace"),
        P("slab", "trace", None),
        P("slab", None, "trace", None),
        P("slab", None, None, "trace"),
        P("slab", None, None, None, "trace"),
    )
    return jax.shard_map(
        on_device,
        mesh=mesh,
        in_specs=placed,
        out_specs=P("slab", None, None, None, "trace"),
        check_vma=False,
    )
```

```python
import jax
import jax.numpy as jnp
from jax import lax
from jax.experimental import pallas as pl
from jax.experimental.pallas import tpu as pltpu
from jax.sharding import PartitionSpec as P

f32 = jnp.float32
bf16 = jnp.bfloat16
small_eps = 1e-06
both_axes = ("slab", "trace")
in_vmem = pl.BlockSpec(memory_space=pltpu.VMEM)
in_smem = pl.BlockSpec(memory_space=pltpu.SMEM)

pieces = 4


def two_parts(x):
    high = x.astype(bf16)
    return high, (x - high.astype(f32)).astype(bf16)


def three_parts(x):
    high = x.astype(bf16)
    rest = x - high.astype(f32)
    middle = rest.astype(bf16)
    return high, middle, (rest - middle.astype(f32)).astype(bf16)


def dot(a, b):
    return jnp.dot(a, b, preferred_element_type=f32)


def times(stacked, high, weight_high, weight_low):
    rows = high.shape[0]
    both = dot(stacked, weight_high)
    return both[:rows] + both[rows:] + dot(high, weight_low)


def complex_times(x, weights):
    high, low = two_parts(x)
    stacked = jnp.concatenate([high, low], axis=0)
    by_re = times(stacked, high, *weights[0])
    by_im = times(stacked, high, *weights[1])
    half = x.shape[0] // 2
    return by_re[:half] - by_im[half:], by_im[:half] + by_re[half:]


def on_odd():
    return lax.rem(lax.axis_index("trace"), 2) == 1


def pick(x, skel_row):
    n, width = x.shape
    rank = skel_row.shape[1]
    rows = lax.broadcasted_iota(jnp.int32, (width, rank), 0)
    chosen = jnp.where(rows == skel_row, 1.0, 0.0).astype(bf16)
    out = dot(jnp.concatenate(three_parts(x), axis=0), chosen)
    out = out[:n] + (out[n : 2 * n] + out[2 * n :])
    lane = lax.broadcasted_iota(jnp.int32, (n, 2 * rank), 1)
    return jnp.where((lane >= rank) == on_odd(), jnp.concatenate([out, out], axis=1), 0.0)


def first_kernel(skel_ref, src_ref, small_ref):
    small_ref[...] = pick(src_ref[...], skel_ref[...])


def split_tiles(slot, tiles_ref, half_refs, held_ref, sems, meanwhile):
    pieces_all, rows, _ = held_ref.shape
    _, tile, _ = tiles_ref.shape
    per = tile // rows
    copies = [
        pltpu.make_async_copy(
            tiles_ref.at[slot * (pieces_all // per) + i // per, pl.ds(i % per * rows, rows)],
            held_ref.at[i],
            sems.at[i],
        )
        for i in range(pieces_all)
    ]
    for copy in copies:
        copy.start()
    meanwhile()
    high_ref, low_ref = half_refs
    for i, copy in enumerate(copies):
        copy.wait()
        high, low = two_parts(held_ref[i])
        place = pl.ds(i % per * rows, rows)
        high_ref[i // per, place] = high
        low_ref[i // per, place] = low


def split_kernel(tiles_ref, high_ref, low_ref, held_ref, sems):
    split_tiles(0, tiles_ref, (high_ref, low_ref), held_ref, sems, lambda: None)


def split_far_kernel(side_ref, coupling_in, basis_in, tiles_ref, *refs):
    coef_ref, base_ref, *half_refs, coupling_ref, basis_ref, far_sems, held_ref, sems = refs
    far_copies = [
        pltpu.make_async_copy(coupling_in, coupling_ref, far_sems.at[0]),
        pltpu.make_async_copy(basis_in, basis_ref, far_sems.at[1]),
    ]

    def meanwhile():
        for copy in far_copies:
            copy.start()

    split_tiles(1, tiles_ref, half_refs, held_ref, sems, meanwhile)
    for copy in far_copies:
        copy.wait()
    split_far(side_ref, coupling_ref, basis_ref, coef_ref, base_ref)


def pair_ways(count):
    return [0, *range(count - 1, 0, -1)]


def split_far(side_ref, coupling_ref, basis_ref, coef_ref, base_ref):
    here = lax.axis_index("trace")
    _, rank, total = coupling_ref.shape
    width = 2 * rank
    half = lax.broadcasted_iota(jnp.int32, (rank, width), 1) // rank
    for j, way in enumerate(pair_ways(total // width)):
        group = (here // 2) ^ way
        block = group * 2 + half
        keep = (block != here) & (block != here + side_ref[0, 0])
        place = pl.ds(pl.multiple_of(group * width, width), width)
        for part in range(2):
            high, low = two_parts(jnp.where(keep, coupling_ref[part, :, place], 0.0).T)
            coef_ref[part, 0, j * width : (j + 1) * width] = high
            coef_ref[part, 1, j * width : (j + 1) * width] = low
    for part in range(2):
        high, low = two_parts(basis_ref[part])
        base_ref[part, 0] = high
        base_ref[part, 1] = low


def add_near(out_ref, start, x, high_ref, low_ref):
    half = x.shape[0] // 2
    re, im = complex_times(x, [(high_ref[p], low_ref[p]) for p in range(2)])
    out_ref[:half] = start[:half] + re
    out_ref[half:] = start[half:] + im


def own_kernel(step, own_ref, src_ref, high_ref, low_ref, out_ref):
    @pl.when(lax.axis_index("slab") == step)
    def _():
        add_near(out_ref, src_ref[...], own_ref[...], high_ref, low_ref)


def beside_kernel(step, side_ref, mate_ref, other_ref, start_ref, high_ref, low_ref, out_ref):
    @pl.when(lax.axis_index("slab") == step)
    def _():
        width = start_ref.shape[1]
        mate = (side_ref[0, 0] < 0) == on_odd()
        x = jnp.where(mate, mate_ref[:, :width], other_ref[:, :width])
        add_near(out_ref, start_ref[...], x, high_ref, low_ref)


def add_far(near_ref, mate_ref, pair_refs, coef_ref, base_ref):
    width = near_ref.shape[1]
    values = jnp.concatenate([mate_ref[:, width:]] + [ref[...] for ref in pair_refs], axis=1)
    weights = [(coef_ref[p, 0], coef_ref[p, 1]) for p in range(2)]
    coef = jnp.concatenate(complex_times(values, weights), axis=0)
    weights = [(base_ref[p, 0], base_ref[p, 1]) for p in range(2)]
    return near_ref[...] + jnp.concatenate(complex_times(coef, weights), axis=0)


def last_kernel(step, old_ref, near_ref, mate_ref, *refs):
    *pair_refs, coef_ref, base_ref, state_ref, energy_ref = refs
    active = lax.axis_index("slab") == step

    @pl.when(active)
    def _():
        state_ref[...] = add_far(near_ref, mate_ref, pair_refs, coef_ref, base_ref)

    @pl.when(jnp.logical_not(active))
    def _():
        state_ref[...] = old_ref[...]

    half = state_ref.shape[0] // 2
    squares = state_ref[...] * state_ref[...]
    each = jnp.sum(squares[:half] + squares[half:], axis=1, keepdims=True)
    energy_ref[...] = jnp.broadcast_to(jnp.broadcast_to(each, (half, 128)).T[:1], energy_ref.shape)


def far_kernel(step, skel_ref, old_ref, near_ref, mate_ref, *refs):
    *pair_refs, coef_ref, base_ref, state_ref, small_ref = refs
    active = lax.axis_index("slab") == step

    @pl.when(active)
    def _():
        new = add_far(near_ref, mate_ref, pair_refs, coef_ref, base_ref)
        state_ref[...] = new
        small_ref[...] = pick(new, skel_ref[...])

    @pl.when(jnp.logical_not(active))
    def _():
        state_ref[...] = old_ref[...]
        small_ref[...] = jnp.zeros_like(small_ref)


def norm_kernel(count, state_ref, sums_ref, out_ref):
    half = state_ref.shape[0] // 2
    total = jnp.sum(sums_ref[...], axis=0, keepdims=True)
    scale = jnp.broadcast_to(1.0 / jnp.sqrt(total / count + small_eps), (128, half)).T[:, :1]
    out_ref[0] = state_ref[:half] * scale
    out_ref[1] = state_ref[half:] * scale


def about(us):
    return pl.CostEstimate(
        flops=int(us * 1.15e9), bytes_accessed=int(us * 3.69e6), transcendentals=0
    )


def across(c, blocks):
    return min(max((c ^ 1) + (2 if c % 2 else -2), 0), blocks - 1)


def call(kernel, name, outs, specs, args, room=6, **more):
    many = isinstance(outs, tuple)
    return pl.pallas_call(
        kernel,
        out_shape=outs,
        in_specs=specs,
        out_specs=[in_vmem] * len(outs) if many else in_vmem,
        compiler_params=pltpu.CompilerParams(vmem_limit_bytes=room << 20),
        name=name,
        **more,
    )(*args)


in_hbm = pl.BlockSpec(memory_space=pl.ANY)


def far_from(x):
    return pltpu.with_memory_space_constraint(x, pltpu.HBM)


def ring_pairs(step, move, slabs, blocks):
    pairs = []
    for place in range(slabs):
        source = (step - 1 + place) % slabs
        target = (source + 1) % slabs
        for c in range(blocks):
            pairs.append((source * blocks + c, target * blocks + (move(c) if place == 0 else c)))
    return pairs


def on_device(near_tiles, near_side, skeleton, far_coupling, far_basis, sources):
    slabs = lax.axis_size("slab")
    blocks = lax.axis_size("trace")
    _, slots, parts, tile, width = near_tiles.shape
    _, _, batches, shots, _ = sources.shape
    rank = skeleton.shape[2]
    rows = batches * shots
    n = parts * rows
    state_type = jax.ShapeDtypeStruct((n, width), f32)
    small_type = jax.ShapeDtypeStruct((n, 2 * rank), f32)

    src = sources.reshape(n, width)
    skel_next = lax.ppermute(
        skeleton.reshape(1, rank), "slab", [((s + 1) % slabs, s) for s in range(slabs)]
    )
    halves = jax.ShapeDtypeStruct((parts, tile, width), bf16)

    held = [
        pltpu.VMEM((parts * pieces, tile // pieces, width), f32),
        pltpu.SemaphoreType.DMA((parts * pieces,)),
    ]

    planes = far_from(near_tiles.reshape(slots * parts, tile, width))
    own_halves = call(
        split_kernel,
        "split_own",
        (halves, halves),
        [in_hbm],
        (planes,),
        scratch_shapes=held,
        cost_estimate=about(2.5),
        room=12,
    )

    def split_rest(planes):
        coef, base, *beside_halves = call(
            split_far_kernel,
            "split_beside",
            (
                jax.ShapeDtypeStruct((parts, 2, blocks * rank, rank), bf16),
                jax.ShapeDtypeStruct((parts, 2, rank, width), bf16),
                halves,
                halves,
            ),
            [in_smem] + [in_hbm] * 3,
            (near_side, far_from(far_coupling[0]), far_from(far_basis[0]), planes),
            scratch_shapes=[
                pltpu.VMEM(far_coupling.shape[1:], f32),
                pltpu.VMEM(far_basis.shape[1:], f32),
                pltpu.SemaphoreType.DMA((2,)),
                *held,
            ],
            cost_estimate=about(2.5),
            room=12,
        )
        return coef, base, beside_halves

    skel_next, *own_halves = lax.optimization_barrier((skel_next, *own_halves))
    state = src
    small = call(first_kernel, "first", small_type, [in_vmem] * 2, (skel_next, src))
    state, small = lax.optimization_barrier((state, small))

    for step in range(1, slabs):

        def send(x, move):
            return lax.ppermute(x, both_axes, ring_pairs(step, move, slabs, blocks))

        def send_pair(x, j):
            return send(x, lambda c: c ^ (2 * j))

        swapped = lax.ppermute(small, "trace", [(c, c ^ 1) for c in range(blocks)])
        pair = small + swapped
        own = send(state, lambda c: c)
        if step == 1:
            own, planes = lax.optimization_barrier((own, planes))
            coef, base, beside_halves = split_rest(planes)
        wide = jnp.concatenate([state, small], axis=1)
        mate = send(wide, lambda c: c ^ 1)
        other = send(state, lambda c: across(c, blocks))
        pairs = [send_pair(pair, way) for way in pair_ways(blocks // 2)[1:]]
        near = call(
            lambda *refs, step=step: own_kernel(step, *refs),
            "own",
            state_type,
            [in_vmem] * 4,
            (own, src, *own_halves),
            cost_estimate=about(5),
        )
        near = call(
            lambda *refs, step=step: beside_kernel(step, *refs),
            "beside",
            state_type,
            [in_smem] + [in_vmem] * 5,
            (near_side, mate, other, near, *beside_halves),
            cost_estimate=about(0.85),
        )
        args = (state, near, mate, *pairs, coef, base)
        if step + 1 < slabs:
            state, small = call(
                lambda *refs, step=step: far_kernel(step, *refs),
                "far",
                (state_type, small_type),
                [in_vmem] * (1 + len(args)),
                (skel_next, *args),
                cost_estimate=about(0.7),
            )
        else:
            state, partial = call(
                lambda *refs, step=step: last_kernel(step, *refs),
                "last",
                (state_type, jax.ShapeDtypeStruct((blocks, rows), f32)),
                [in_vmem] * len(args),
                args,
                cost_estimate=about(0.7),
            )

    sums = lax.all_to_all(partial, "trace", 0, 0)
    normed = call(
        lambda *refs: norm_kernel(float(parts * width * blocks), *refs),
        "norm",
        jax.ShapeDtypeStruct((parts, rows, width), f32),
        [in_vmem] * 2,
        (state, sums),
    )
    return normed.reshape(sources.shape)


def solution(mesh):
    placed = (
        P("slab", None, None, None, "trace"),
        P("slab", "trace"),
        P("slab", "trace", None),
        P("slab", None, "trace", None),
        P("slab", None, None, "trace"),
        P("slab", None, None, None, "trace"),
    )
    return jax.shard_map(
        on_device,
        mesh=mesh,
        in_specs=placed,
        out_specs=P("slab", None, None, None, "trace"),
        check_vma=False,
    )
```

```python
import jax
import jax.numpy as jnp
from jax import lax
from jax.experimental import pallas as pl
from jax.experimental.pallas import tpu as pltpu
from jax.sharding import PartitionSpec as P

f32 = jnp.float32
bf16 = jnp.bfloat16
small_eps = 1e-06
both_axes = ("slab", "trace")
in_vmem = pl.BlockSpec(memory_space=pltpu.VMEM)
in_smem = pl.BlockSpec(memory_space=pltpu.SMEM)

pieces = 4


def two_parts(x):
    high = x.astype(bf16)
    return high, (x - high.astype(f32)).astype(bf16)


def three_parts(x):
    high = x.astype(bf16)
    rest = x - high.astype(f32)
    middle = rest.astype(bf16)
    return high, middle, (rest - middle.astype(f32)).astype(bf16)


def dot(a, b):
    return jnp.dot(a, b, preferred_element_type=f32)


def times(stacked, high, weight_high, weight_low):
    rows = high.shape[0]
    both = dot(stacked, weight_high)
    return both[:rows] + both[rows:] + dot(high, weight_low)


def complex_times(x, weights):
    high, low = two_parts(x)
    stacked = jnp.concatenate([high, low], axis=0)
    by_re = times(stacked, high, *weights[0])
    by_im = times(stacked, high, *weights[1])
    half = x.shape[0] // 2
    return by_re[:half] - by_im[half:], by_im[:half] + by_re[half:]


def on_odd():
    return lax.rem(lax.axis_index("trace"), 2) == 1


def pick(x, skel_row):
    n, width = x.shape
    rank = skel_row.shape[1]
    rows = lax.broadcasted_iota(jnp.int32, (width, rank), 0)
    chosen = jnp.where(rows == skel_row, 1.0, 0.0).astype(bf16)
    out = dot(jnp.concatenate(three_parts(x), axis=0), chosen)
    out = out[:n] + (out[n : 2 * n] + out[2 * n :])
    lane = lax.broadcasted_iota(jnp.int32, (n, 2 * rank), 1)
    return jnp.where((lane >= rank) == on_odd(), jnp.concatenate([out, out], axis=1), 0.0)


def first_kernel(skel_ref, src_ref, small_ref):
    small_ref[...] = pick(src_ref[...], skel_ref[...])


def split_tiles(slot, tiles_ref, half_refs, held_ref, sems, meanwhile):
    pieces_all, rows, _ = held_ref.shape
    _, tile, _ = tiles_ref.shape
    per = tile // rows
    copies = [
        pltpu.make_async_copy(
            tiles_ref.at[slot * (pieces_all // per) + i // per, pl.ds(i % per * rows, rows)],
            held_ref.at[i],
            sems.at[i],
        )
        for i in range(pieces_all)
    ]
    for copy in copies:
        copy.start()
    meanwhile()
    high_ref, low_ref = half_refs
    for i, copy in enumerate(copies):
        copy.wait()
        high, low = two_parts(held_ref[i])
        place = pl.ds(i % per * rows, rows)
        high_ref[i // per, place] = high
        low_ref[i // per, place] = low


def split_kernel(tiles_ref, high_ref, low_ref, held_ref, sems):
    split_tiles(0, tiles_ref, (high_ref, low_ref), held_ref, sems, lambda: None)


def split_far_kernel(side_ref, coupling_in, basis_in, tiles_ref, *refs):
    coef_ref, base_ref, *half_refs, coupling_ref, basis_ref, far_sems, held_ref, sems = refs
    far_copies = [
        pltpu.make_async_copy(coupling_in, coupling_ref, far_sems.at[0]),
        pltpu.make_async_copy(basis_in, basis_ref, far_sems.at[1]),
    ]

    def meanwhile():
        for copy in far_copies:
            copy.start()

    split_tiles(1, tiles_ref, half_refs, held_ref, sems, meanwhile)
    for copy in far_copies:
        copy.wait()
    split_far(side_ref, coupling_ref, basis_ref, coef_ref, base_ref)


def pair_ways(count):
    return [0, *range(count - 1, 0, -1)]


def split_far(side_ref, coupling_ref, basis_ref, coef_ref, base_ref):
    here = lax.axis_index("trace")
    _, rank, total = coupling_ref.shape
    width = 2 * rank
    half = lax.broadcasted_iota(jnp.int32, (rank, width), 1) // rank
    for j, way in enumerate(pair_ways(total // width)):
        group = (here // 2) ^ way
        block = group * 2 + half
        keep = (block != here) & (block != here + side_ref[0, 0])
        place = pl.ds(pl.multiple_of(group * width, width), width)
        for part in range(2):
            high, low = two_parts(jnp.where(keep, coupling_ref[part, :, place], 0.0).T)
            coef_ref[part, 0, j * width : (j + 1) * width] = high
            coef_ref[part, 1, j * width : (j + 1) * width] = low
    for part in range(2):
        high, low = two_parts(basis_ref[part])
        base_ref[part, 0] = high
        base_ref[part, 1] = low


def add_near(out_ref, start, x, high_ref, low_ref):
    half = x.shape[0] // 2
    re, im = complex_times(x, [(high_ref[p], low_ref[p]) for p in range(2)])
    out_ref[:half] = start[:half] + re
    out_ref[half:] = start[half:] + im


def own_kernel(step, own_ref, src_ref, high_ref, low_ref, out_ref):
    @pl.when(lax.axis_index("slab") == step)
    def _():
        add_near(out_ref, src_ref[...], own_ref[...], high_ref, low_ref)


def beside_kernel(step, side_ref, mate_ref, other_ref, start_ref, high_ref, low_ref, out_ref):
    @pl.when(lax.axis_index("slab") == step)
    def _():
        width = start_ref.shape[1]
        mate = (side_ref[0, 0] < 0) == on_odd()
        x = jnp.where(mate, mate_ref[:, :width], other_ref[:, :width])
        add_near(out_ref, start_ref[...], x, high_ref, low_ref)


def add_far(near_ref, mate_ref, pair_refs, coef_ref, base_ref):
    width = near_ref.shape[1]
    values = jnp.concatenate([mate_ref[:, width:]] + [ref[...] for ref in pair_refs], axis=1)
    weights = [(coef_ref[p, 0], coef_ref[p, 1]) for p in range(2)]
    coef = jnp.concatenate(complex_times(values, weights), axis=0)
    weights = [(base_ref[p, 0], base_ref[p, 1]) for p in range(2)]
    return near_ref[...] + jnp.concatenate(complex_times(coef, weights), axis=0)


def last_kernel(step, old_ref, near_ref, mate_ref, *refs):
    *pair_refs, coef_ref, base_ref, state_ref, energy_ref = refs
    active = lax.axis_index("slab") == step

    @pl.when(active)
    def _():
        state_ref[...] = add_far(near_ref, mate_ref, pair_refs, coef_ref, base_ref)

    @pl.when(jnp.logical_not(active))
    def _():
        state_ref[...] = old_ref[...]

    half = state_ref.shape[0] // 2
    squares = state_ref[...] * state_ref[...]
    each = jnp.sum(squares[:half] + squares[half:], axis=1, keepdims=True)
    energy_ref[...] = jnp.broadcast_to(jnp.broadcast_to(each, (half, 128)).T[:1], energy_ref.shape)


def far_kernel(step, skel_ref, old_ref, near_ref, mate_ref, *refs):
    *pair_refs, coef_ref, base_ref, state_ref, small_ref = refs
    active = lax.axis_index("slab") == step

    @pl.when(active)
    def _():
        new = add_far(near_ref, mate_ref, pair_refs, coef_ref, base_ref)
        state_ref[...] = new
        small_ref[...] = pick(new, skel_ref[...])

    @pl.when(jnp.logical_not(active))
    def _():
        state_ref[...] = old_ref[...]
        small_ref[...] = jnp.zeros_like(small_ref)


def norm_kernel(count, state_ref, sums_ref, out_ref):
    half = state_ref.shape[0] // 2
    total = jnp.sum(sums_ref[...], axis=0, keepdims=True)
    scale = jnp.broadcast_to(1.0 / jnp.sqrt(total / count + small_eps), (128, half)).T[:, :1]
    out_ref[0] = state_ref[:half] * scale
    out_ref[1] = state_ref[half:] * scale


def about(us):
    return pl.CostEstimate(
        flops=int(us * 1.15e9), bytes_accessed=int(us * 3.69e6), transcendentals=0
    )


def across(c, blocks):
    return min(max((c ^ 1) + (2 if c % 2 else -2), 0), blocks - 1)


def call(kernel, name, outs, specs, args, room=6, **more):
    many = isinstance(outs, tuple)
    return pl.pallas_call(
        kernel,
        out_shape=outs,
        in_specs=specs,
        out_specs=[in_vmem] * len(outs) if many else in_vmem,
        compiler_params=pltpu.CompilerParams(vmem_limit_bytes=room << 20),
        name=name,
        **more,
    )(*args)


in_hbm = pl.BlockSpec(memory_space=pl.ANY)


def far_from(x):
    return pltpu.with_memory_space_constraint(x, pltpu.HBM)


def ring_pairs(step, move, slabs, blocks):
    pairs = []
    order = [step - 1, step] + [(step - 2 - i) % slabs for i in range(slabs - 2)]
    for place in range(slabs):
        source, target = order[place], order[(place + 1) % slabs]
        for c in range(blocks):
            pairs.append((source * blocks + c, target * blocks + (move(c) if place == 0 else c)))
    return pairs


def on_device(near_tiles, near_side, skeleton, far_coupling, far_basis, sources):
    slabs = lax.axis_size("slab")
    blocks = lax.axis_size("trace")
    _, slots, parts, tile, width = near_tiles.shape
    _, _, batches, shots, _ = sources.shape
    rank = skeleton.shape[2]
    rows = batches * shots
    n = parts * rows
    state_type = jax.ShapeDtypeStruct((n, width), f32)
    small_type = jax.ShapeDtypeStruct((n, 2 * rank), f32)

    src = sources.reshape(n, width)
    skel_next = lax.ppermute(
        skeleton.reshape(1, rank), "slab", [((s + 1) % slabs, s) for s in range(slabs)]
    )
    halves = jax.ShapeDtypeStruct((parts, tile, width), bf16)

    held = [
        pltpu.VMEM((parts * pieces, tile // pieces, width), f32),
        pltpu.SemaphoreType.DMA((parts * pieces,)),
    ]

    planes = far_from(near_tiles.reshape(slots * parts, tile, width))
    own_halves = call(
        split_kernel,
        "split_own",
        (halves, halves),
        [in_hbm],
        (planes,),
        scratch_shapes=held,
        cost_estimate=about(2.5),
        room=12,
    )

    def split_rest(planes):
        coef, base, *beside_halves = call(
            split_far_kernel,
            "split_beside",
            (
                jax.ShapeDtypeStruct((parts, 2, blocks * rank, rank), bf16),
                jax.ShapeDtypeStruct((parts, 2, rank, width), bf16),
                halves,
                halves,
            ),
            [in_smem] + [in_hbm] * 3,
            (near_side, far_from(far_coupling[0]), far_from(far_basis[0]), planes),
            scratch_shapes=[
                pltpu.VMEM(far_coupling.shape[1:], f32),
                pltpu.VMEM(far_basis.shape[1:], f32),
                pltpu.SemaphoreType.DMA((2,)),
                *held,
            ],
            cost_estimate=about(2.5),
            room=12,
        )
        return coef, base, beside_halves

    skel_next, *own_halves = lax.optimization_barrier((skel_next, *own_halves))
    state = src
    small = call(first_kernel, "first", small_type, [in_vmem] * 2, (skel_next, src))
    state, small = lax.optimization_barrier((state, small))

    for step in range(1, slabs):

        def send(x, move):
            return lax.ppermute(x, both_axes, ring_pairs(step, move, slabs, blocks))

        def send_pair(x, j):
            return send(x, lambda c: c ^ (2 * j))

        swapped = lax.ppermute(small, "trace", [(c, c ^ 1) for c in range(blocks)])
        pair = small + swapped
        own = send(state, lambda c: c)
        if step == 1:
            own, planes = lax.optimization_barrier((own, planes))
            coef, base, beside_halves = split_rest(planes)
        wide = jnp.concatenate([state, small], axis=1)
        mate = send(wide, lambda c: c ^ 1)
        other = send(state, lambda c: across(c, blocks))
        pairs = [send_pair(pair, way) for way in pair_ways(blocks // 2)[1:]]
        near = call(
            lambda *refs, step=step: own_kernel(step, *refs),
            "own",
            state_type,
            [in_vmem] * 4,
            (own, src, *own_halves),
            cost_estimate=about(5),
        )
        near = call(
            lambda *refs, step=step: beside_kernel(step, *refs),
            "beside",
            state_type,
            [in_smem] + [in_vmem] * 5,
            (near_side, mate, other, near, *beside_halves),
            cost_estimate=about(0.85),
        )
        args = (state, near, mate, *pairs, coef, base)
        if step + 1 < slabs:
            state, small = call(
                lambda *refs, step=step: far_kernel(step, *refs),
                "far",
                (state_type, small_type),
                [in_vmem] * (1 + len(args)),
                (skel_next, *args),
                cost_estimate=about(0.7),
            )
        else:
            state, partial = call(
                lambda *refs, step=step: last_kernel(step, *refs),
                "last",
                (state_type, jax.ShapeDtypeStruct((blocks, rows), f32)),
                [in_vmem] * len(args),
                args,
                cost_estimate=about(0.7),
            )

    sums = lax.all_to_all(partial, "trace", 0, 0)
    normed = call(
        lambda *refs: norm_kernel(float(parts * width * blocks), *refs),
        "norm",
        jax.ShapeDtypeStruct((parts, rows, width), f32),
        [in_vmem] * 2,
        (state, sums),
    )
    return normed.reshape(sources.shape)


def solution(mesh):
    placed = (
        P("slab", None, None, None, "trace"),
        P("slab", "trace"),
        P("slab", "trace", None),
        P("slab", None, "trace", None),
        P("slab", None, None, "trace"),
        P("slab", None, None, None, "trace"),
    )
    return jax.shard_map(
        on_device,
        mesh=mesh,
        in_specs=placed,
        out_specs=P("slab", None, None, None, "trace"),
        check_vma=False,
    )
```

```python
import jax
import jax.numpy as jnp
from jax import lax
from jax.experimental import pallas as pl
from jax.experimental.pallas import tpu as pltpu
from jax.sharding import PartitionSpec as P

f32 = jnp.float32
bf16 = jnp.bfloat16
small_eps = 1e-06
both_axes = ("slab", "trace")
in_vmem = pl.BlockSpec(memory_space=pltpu.VMEM)
in_smem = pl.BlockSpec(memory_space=pltpu.SMEM)

pieces = 4


def two_parts(x):
    high = x.astype(bf16)
    return high, (x - high.astype(f32)).astype(bf16)


def three_parts(x):
    high = x.astype(bf16)
    rest = x - high.astype(f32)
    middle = rest.astype(bf16)
    return high, middle, (rest - middle.astype(f32)).astype(bf16)


def dot(a, b):
    return jnp.dot(a, b, preferred_element_type=f32)


def times(stacked, high, weight_high, weight_low):
    rows = high.shape[0]
    both = dot(stacked, weight_high)
    return both[:rows] + both[rows:] + dot(high, weight_low)


def complex_times(x, weights):
    high, low = two_parts(x)
    stacked = jnp.concatenate([high, low], axis=0)
    by_re = times(stacked, high, *weights[0])
    by_im = times(stacked, high, *weights[1])
    half = x.shape[0] // 2
    return by_re[:half] - by_im[half:], by_im[:half] + by_re[half:]


def on_odd():
    return lax.rem(lax.axis_index("trace"), 2) == 1


def pick(x, skel_row):
    n, width = x.shape
    rank = skel_row.shape[1]
    rows = lax.broadcasted_iota(jnp.int32, (width, rank), 0)
    chosen = jnp.where(rows == skel_row, 1.0, 0.0).astype(bf16)
    out = dot(jnp.concatenate(three_parts(x), axis=0), chosen)
    out = out[:n] + (out[n : 2 * n] + out[2 * n :])
    lane = lax.broadcasted_iota(jnp.int32, (n, 2 * rank), 1)
    return jnp.where((lane >= rank) == on_odd(), jnp.concatenate([out, out], axis=1), 0.0)


def first_kernel(skel_ref, src_ref, small_ref):
    small_ref[...] = pick(src_ref[...], skel_ref[...])


def split_tiles(slot, tiles_ref, half_refs, held_ref, sems, meanwhile):
    pieces_all, rows, _ = held_ref.shape
    _, tile, _ = tiles_ref.shape
    per = tile // rows
    copies = [
        pltpu.make_async_copy(
            tiles_ref.at[slot * (pieces_all // per) + i // per, pl.ds(i % per * rows, rows)],
            held_ref.at[i],
            sems.at[i],
        )
        for i in range(pieces_all)
    ]
    for copy in copies:
        copy.start()
    meanwhile()
    high_ref, low_ref = half_refs
    for i, copy in enumerate(copies):
        copy.wait()
        high, low = two_parts(held_ref[i])
        place = pl.ds(i % per * rows, rows)
        high_ref[i // per, place] = high
        low_ref[i // per, place] = low


def split_kernel(tiles_ref, high_ref, low_ref, held_ref, sems):
    split_tiles(0, tiles_ref, (high_ref, low_ref), held_ref, sems, lambda: None)


def split_far_kernel(side_ref, coupling_in, basis_in, tiles_ref, *refs):
    coef_ref, base_ref, *half_refs, coupling_ref, basis_ref, far_sems, held_ref, sems = refs
    far_copies = [
        pltpu.make_async_copy(coupling_in, coupling_ref, far_sems.at[0]),
        pltpu.make_async_copy(basis_in, basis_ref, far_sems.at[1]),
    ]

    def meanwhile():
        for copy in far_copies:
            copy.start()

    split_tiles(1, tiles_ref, half_refs, held_ref, sems, meanwhile)
    for copy in far_copies:
        copy.wait()
    split_far(side_ref, coupling_ref, basis_ref, coef_ref, base_ref)


def pair_ways(count):
    return [0, *range(count - 1, 0, -1)]


def split_far(side_ref, coupling_ref, basis_ref, coef_ref, base_ref):
    here = lax.axis_index("trace")
    _, rank, total = coupling_ref.shape
    width = 2 * rank
    half = lax.broadcasted_iota(jnp.int32, (rank, width), 1) // rank
    for j, way in enumerate(pair_ways(total // width)):
        group = (here // 2) ^ way
        block = group * 2 + half
        keep = (block != here) & (block != here + side_ref[0, 0])
        place = pl.ds(pl.multiple_of(group * width, width), width)
        for part in range(2):
            high, low = two_parts(jnp.where(keep, coupling_ref[part, :, place], 0.0).T)
            coef_ref[part, 0, j * width : (j + 1) * width] = high
            coef_ref[part, 1, j * width : (j + 1) * width] = low
    for part in range(2):
        high, low = two_parts(basis_ref[part])
        base_ref[part, 0] = high
        base_ref[part, 1] = low


def add_near(out_ref, start, x, high_ref, low_ref):
    half = x.shape[0] // 2
    re, im = complex_times(x, [(high_ref[p], low_ref[p]) for p in range(2)])
    out_ref[:half] = start[:half] + re
    out_ref[half:] = start[half:] + im


def own_kernel(step, own_ref, src_ref, high_ref, low_ref, out_ref):
    @pl.when(lax.axis_index("slab") == step)
    def _():
        add_near(out_ref, src_ref[...], own_ref[...], high_ref, low_ref)


def beside_kernel(step, side_ref, mate_ref, other_ref, start_ref, high_ref, low_ref, out_ref):
    @pl.when(lax.axis_index("slab") == step)
    def _():
        width = start_ref.shape[1]
        mate = (side_ref[0, 0] < 0) == on_odd()
        x = jnp.where(mate, mate_ref[:, :width], other_ref[:, :width])
        add_near(out_ref, start_ref[...], x, high_ref, low_ref)


def add_far(near_ref, mate_ref, pair_refs, coef_ref, base_ref):
    width = near_ref.shape[1]
    values = jnp.concatenate([mate_ref[:, width:]] + [ref[...] for ref in pair_refs], axis=1)
    weights = [(coef_ref[p, 0], coef_ref[p, 1]) for p in range(2)]
    coef = jnp.concatenate(complex_times(values, weights), axis=0)
    weights = [(base_ref[p, 0], base_ref[p, 1]) for p in range(2)]
    return near_ref[...] + jnp.concatenate(complex_times(coef, weights), axis=0)


def last_kernel(step, old_ref, near_ref, mate_ref, *refs):
    *pair_refs, coef_ref, base_ref, state_ref, energy_ref = refs
    active = lax.axis_index("slab") == step

    @pl.when(active)
    def _():
        state_ref[...] = add_far(near_ref, mate_ref, pair_refs, coef_ref, base_ref)

    @pl.when(jnp.logical_not(active))
    def _():
        state_ref[...] = old_ref[...]

    half = state_ref.shape[0] // 2
    squares = state_ref[...] * state_ref[...]
    each = jnp.sum(squares[:half] + squares[half:], axis=1, keepdims=True)
    energy_ref[...] = jnp.broadcast_to(jnp.broadcast_to(each, (half, 128)).T[:1], energy_ref.shape)


def far_kernel(step, skel_ref, old_ref, near_ref, mate_ref, *refs):
    *pair_refs, coef_ref, base_ref, state_ref, small_ref = refs
    active = lax.axis_index("slab") == step

    @pl.when(active)
    def _():
        new = add_far(near_ref, mate_ref, pair_refs, coef_ref, base_ref)
        state_ref[...] = new
        small_ref[...] = pick(new, skel_ref[...])

    @pl.when(jnp.logical_not(active))
    def _():
        state_ref[...] = old_ref[...]
        small_ref[...] = jnp.zeros_like(small_ref)


def norm_kernel(count, state_ref, sums_ref, out_ref):
    half = state_ref.shape[0] // 2
    total = jnp.sum(sums_ref[...], axis=0, keepdims=True)
    scale = jnp.broadcast_to(1.0 / jnp.sqrt(total / count + small_eps), (128, half)).T[:, :1]
    out_ref[0] = state_ref[:half] * scale
    out_ref[1] = state_ref[half:] * scale


def about(us):
    return pl.CostEstimate(
        flops=int(us * 1.15e9), bytes_accessed=int(us * 3.69e6), transcendentals=0
    )


def across(c, blocks):
    return min(max((c ^ 1) + (2 if c % 2 else -2), 0), blocks - 1)


def call(kernel, name, outs, specs, args, room=6, **more):
    many = isinstance(outs, tuple)
    return pl.pallas_call(
        kernel,
        out_shape=outs,
        in_specs=specs,
        out_specs=[in_vmem] * len(outs) if many else in_vmem,
        compiler_params=pltpu.CompilerParams(vmem_limit_bytes=room << 20),
        name=name,
        **more,
    )(*args)


in_hbm = pl.BlockSpec(memory_space=pl.ANY)


def far_from(x):
    return pltpu.with_memory_space_constraint(x, pltpu.HBM)


def ring_pairs(step, move, slabs, blocks):
    pairs = []
    order = [step - 1, step] + [(step - 2 - i) % slabs for i in range(slabs - 2)]
    for place in range(slabs):
        source, target = order[place], order[(place + 1) % slabs]
        for c in range(blocks):
            pairs.append((source * blocks + c, target * blocks + (move(c) if place == 0 else c)))
    return pairs


def swap_pairs(step, move, slabs, blocks):
    rest = [(step + 1 + i) % slabs for i in range(slabs - 2)]
    pairs = []
    for place, (one, two) in enumerate([(step - 1, step), *zip(rest[::2], rest[1::2])]):
        for c in range(blocks):
            to = move(c) if place == 0 else c
            pairs += [(one * blocks + c, two * blocks + to), (two * blocks + to, one * blocks + c)]
    return pairs


def on_device(near_tiles, near_side, skeleton, far_coupling, far_basis, sources):
    slabs = lax.axis_size("slab")
    blocks = lax.axis_size("trace")
    _, slots, parts, tile, width = near_tiles.shape
    _, _, batches, shots, _ = sources.shape
    rank = skeleton.shape[2]
    rows = batches * shots
    n = parts * rows
    state_type = jax.ShapeDtypeStruct((n, width), f32)
    small_type = jax.ShapeDtypeStruct((n, 2 * rank), f32)

    src = sources.reshape(n, width)
    skel_next = lax.ppermute(
        skeleton.reshape(1, rank), "slab", [((s + 1) % slabs, s) for s in range(slabs)]
    )
    halves = jax.ShapeDtypeStruct((parts, tile, width), bf16)

    held = [
        pltpu.VMEM((parts * pieces, tile // pieces, width), f32),
        pltpu.SemaphoreType.DMA((parts * pieces,)),
    ]

    planes = far_from(near_tiles.reshape(slots * parts, tile, width))
    own_halves = call(
        split_kernel,
        "split_own",
        (halves, halves),
        [in_hbm],
        (planes,),
        scratch_shapes=held,
        cost_estimate=about(2.5),
        room=12,
    )

    def split_rest(planes):
        coef, base, *beside_halves = call(
            split_far_kernel,
            "split_beside",
            (
                jax.ShapeDtypeStruct((parts, 2, blocks * rank, rank), bf16),
                jax.ShapeDtypeStruct((parts, 2, rank, width), bf16),
                halves,
                halves,
            ),
            [in_smem] + [in_hbm] * 3,
            (near_side, far_from(far_coupling[0]), far_from(far_basis[0]), planes),
            scratch_shapes=[
                pltpu.VMEM(far_coupling.shape[1:], f32),
                pltpu.VMEM(far_basis.shape[1:], f32),
                pltpu.SemaphoreType.DMA((2,)),
                *held,
            ],
            cost_estimate=about(2.5),
            room=12,
        )
        return coef, base, beside_halves

    skel_next, *own_halves = lax.optimization_barrier((skel_next, *own_halves))
    state = src
    small = call(first_kernel, "first", small_type, [in_vmem] * 2, (skel_next, src))
    state, small = lax.optimization_barrier((state, small))

    for step in range(1, slabs):

        def send(x, move):
            return lax.ppermute(x, both_axes, ring_pairs(step, move, slabs, blocks))

        def trade(x, move):
            return lax.ppermute(x, both_axes, swap_pairs(step, move, slabs, blocks))

        def send_pair(x, j):
            return send(x, lambda c: c ^ (2 * j))

        swapped = lax.ppermute(small, "trace", [(c, c ^ 1) for c in range(blocks)])
        pair = small + swapped
        own = (trade if step % 2 else send)(state, lambda c: c)
        if step == 1:
            own, planes = lax.optimization_barrier((own, planes))
            coef, base, beside_halves = split_rest(planes)
        wide = jnp.concatenate([state, small], axis=1)
        mate = (trade if step % 2 else send)(wide, lambda c: c ^ 1)
        other = send(state, lambda c: across(c, blocks))
        pairs = [send_pair(pair, way) for way in pair_ways(blocks // 2)[1:]]
        near = call(
            lambda *refs, step=step: own_kernel(step, *refs),
            "own",
            state_type,
            [in_vmem] * 4,
            (own, src, *own_halves),
            cost_estimate=about(5),
        )
        near = call(
            lambda *refs, step=step: beside_kernel(step, *refs),
            "beside",
            state_type,
            [in_smem] + [in_vmem] * 5,
            (near_side, mate, other, near, *beside_halves),
            cost_estimate=about(0.85),
        )
        args = (state, near, mate, *pairs, coef, base)
        if step + 1 < slabs:
            state, small = call(
                lambda *refs, step=step: far_kernel(step, *refs),
                "far",
                (state_type, small_type),
                [in_vmem] * (1 + len(args)),
                (skel_next, *args),
                cost_estimate=about(0.7),
            )
        else:
            state, partial = call(
                lambda *refs, step=step: last_kernel(step, *refs),
                "last",
                (state_type, jax.ShapeDtypeStruct((blocks, rows), f32)),
                [in_vmem] * len(args),
                args,
                cost_estimate=about(0.7),
            )

    sums = lax.all_to_all(partial, "trace", 0, 0)
    normed = call(
        lambda *refs: norm_kernel(float(parts * width * blocks), *refs),
        "norm",
        jax.ShapeDtypeStruct((parts, rows, width), f32),
        [in_vmem] * 2,
        (state, sums),
    )
    return normed.reshape(sources.shape)


def solution(mesh):
    placed = (
        P("slab", None, None, None, "trace"),
        P("slab", "trace"),
        P("slab", "trace", None),
        P("slab", None, "trace", None),
        P("slab", None, None, "trace"),
        P("slab", None, None, None, "trace"),
    )
    return jax.shard_map(
        on_device,
        mesh=mesh,
        in_specs=placed,
        out_specs=P("slab", None, None, None, "trace"),
        check_vma=False,
    )
```
